32 devices in a mesh: row: 8 (over z, core), col: 4 (over y, x).
Axes of the slice: x: 2, y: 2, z: 4, core: 2. Of those that a mesh axis runs over, the one named last changes fastest.
Arguments:
- momentum: bfloat16 [12288, 26624], P('row', 'col'), may hold values from -13 to 13
- gradient: bfloat16 [12288, 26624], P('row', 'col'), may hold values from -0.59765625 to 0.59765625
- basis: float32 [256, 26624], P('row', 'col'), may hold values from -0.0390625 to 0.0390625
Outputs:
- momentum_new: bfloat16 [12288, 26624], P('row', 'col')
- basis_new: float32 [256, 26624], P('row', 'col')
- left_factor: float32 [12288, 256], P(('row', 'col'))
The draws below stay inside these ranges and needn't reach their ends.
All inputs are finite; a program needn't handle non-finite values.
Results may differ from the reference program's by a relative error of at most 0.0073.
The reference program's roundings to bfloat16 on the way (of `buffer`, `directions` and `left_half`) count: a program that leaves them out, or rounds other values in their place, can miss the bound.
Values may be sent and summed in bfloat16 or wider, within the bound.
A program may use at most 192 MiB of HBM per device.

```python
import math
import jax
import jax.numpy as jnp
from jax import lax

ROWS = 12288
COLS = 26624
RANK = 256
POWER = 2


def draw_momentum(key, part):
    key = jax.random.fold_in(key, 11)
    key_label, key_table, key_scale, key_noise, key_group = jax.random.split(key, 5)
    groups = 5 * RANK // 4
    labels = jax.random.randint(key_label, (ROWS,), 0, groups)
    scales = jnp.exp(jax.random.uniform(key_scale, (groups,), jnp.float32, 0.0, math.log(12.0)))
    place = jnp.arange(COLS, dtype=jnp.float32) / COLS
    group_index = jnp.arange(COLS, dtype=jnp.int32) * 64 // COLS
    group_factor = jnp.exp(jax.random.uniform(key_group, (64,), jnp.float32, 0.0, math.log(2.5)))
    ramp = jnp.exp(math.log(4.0) * (place - 1.0))
    row_table = jnp.clip(jax.random.normal(key_table, (groups, COLS), jnp.float32), -4.0, 4.0)
    noise_part = 0.25 * jnp.clip(jax.random.normal(key_noise, (ROWS, COLS), jnp.float32), -4.0, 4.0)
    column_scale = 0.0875 * ramp * jnp.take(group_factor, group_index)
    shaped = row_table * scales[:, None]
    return ((jnp.take(shaped, labels, axis=0) + noise_part) * column_scale[None, :]).astype(jnp.bfloat16)


def block_scale(rng, shape, cuts, smallest, high):
    factor_of = 1.0
    for axis_at, shards_of in cuts:
        heights = jax.random.uniform(jax.random.fold_in(jax.random.fold_in(rng, 6), axis_at), (shards_of,), jnp.float32, smallest / len(cuts), high / len(cuts))
        factor_of = factor_of * jnp.repeat(jnp.exp(heights), shape[axis_at] // shards_of).reshape((-1,) + (1,) * (len(shape) - 1 - axis_at))
    return factor_of


def normal_values(own_key, extent, scale, most, cuts=(), held_as=jnp.bfloat16):
    drawn = jax.random.normal(own_key, extent, jnp.float32) * scale
    if len(cuts) > 0:
        drawn = block_scale(own_key, extent, cuts, -0.22, 0.18) * drawn
    return jnp.clip(drawn, min=-most, max=most).astype(held_as)


def setup_inputs(seed: int = 0) -> dict:
    key_of = jax.random.split(jax.random.key(seed), 4)
    momentum = draw_momentum(jax.random.fold_in(key_of[3], 71), 0)
    gradient = normal_values(key_of[1], (ROWS, COLS), 0.1, 0.59765625, ((0, 8), (1, 4)))
    basis = normal_values(key_of[2], (RANK, COLS), COLS ** -0.5, 0.0390625, ((0, 8), (1, 4)), jnp.float32)
    return dict(momentum=momentum, gradient=gradient, basis=basis)


decay_rate = 0.95
epsilon = 1e-06

def reference(momentum, gradient, basis):
    buffer = (momentum.astype(jnp.float32) + gradient.astype(jnp.float32)).astype(jnp.bfloat16)
    directions = basis.astype(jnp.bfloat16)
    for step in range(POWER):
        power = lax.dot_general(buffer.astype(jnp.float32), directions.astype(jnp.float32), (((1,), (1,)), ((), ())), preferred_element_type=jnp.float32)
        gram = jnp.dot(power.T, power, precision=lax.Precision.HIGHEST)
        chol = jnp.linalg.cholesky(gram)
        left_factor = lax.linalg.triangular_solve(chol, power, left_side=False, lower=True, transpose_a=True)
        left_half = left_factor.astype(jnp.bfloat16)
        right = lax.dot_general(left_half.astype(jnp.float32), buffer.astype(jnp.float32), (((0,), (0,)), ((), ())), preferred_element_type=jnp.float32)
        directions = right.astype(jnp.bfloat16)
    squares = lax.optimization_barrier(jnp.sum(right * right, axis=1, keepdims=True))
    basis_new = right / jnp.sqrt(squares / COLS + epsilon)
    update = jnp.dot(left_half.astype(jnp.float32), directions.astype(jnp.float32), preferred_element_type=jnp.float32)
    momentum_new = (buffer.astype(jnp.float32) - (1.0 - decay_rate) * update).astype(jnp.bfloat16)
    return (momentum_new, basis_new, left_factor)
```

```python
import functools

import jax
import jax.numpy as jnp
from jax import lax
from jax.experimental import pallas as pl
from jax.experimental.pallas import tpu as pltpu
from jax.sharding import PartitionSpec as P

COLS = 26624
POWER = 2
BLOCK = 128
PANEL = 8
MESH = pl.DeviceIdType.MESH
HIGHEST = lax.Precision.HIGHEST


decay_rate = 0.95
epsilon = 1e-06


def dot(a, b, ca, cb, precision=HIGHEST):
    return lax.dot_general(
        a, b, (((ca,), (cb,)), ((), ())), precision=precision, preferred_element_type=jnp.float32
    )


def inverse_factor(a, work, inv):
    n = BLOCK
    work[...] = a
    rows = lax.broadcasted_iota(jnp.int32, (n, n), 0)
    lanes = lax.broadcasted_iota(jnp.int32, (n, n), 1)
    inv[...] = jnp.where(rows == lanes, 1.0, 0.0).astype(jnp.float32)
    sub = lax.broadcasted_iota(jnp.int32, (PANEL, n), 0)
    lane = lax.broadcasted_iota(jnp.int32, (PANEL, n), 1)

    def panel(p, carry):
        at = pl.multiple_of(p * PANEL, PANEL)
        pa = work[pl.ds(at, PANEL), :]
        pm = inv[pl.ds(at, PANEL), :]
        d = pltpu.roll(pa, n - at, 1)
        for k in range(PANEL):
            pivot = jnp.broadcast_to(d[k : k + 1, k : k + 1], (PANEL, n))
            r = lax.rsqrt(pivot)
            r = r * (1.5 - 0.5 * (pivot * r) * r)
            column = jnp.broadcast_to(d[:, k : k + 1], (PANEL, n)) * r
            dk = jnp.broadcast_to(d[k : k + 1, :], (PANEL, n)) * r
            ak = jnp.broadcast_to(pa[k : k + 1, :], (PANEL, n)) * r
            mk = jnp.broadcast_to(pm[k : k + 1, :], (PANEL, n)) * r
            below = sub > k
            here = sub == k
            d = jnp.where(here, dk, jnp.where(below, d - column * dk, d))
            pa = jnp.where(here, ak, jnp.where(below, pa - column * ak, pa))
            pm = jnp.where(here, mk, jnp.where(below, pm - column * mk, pm))
        inv[pl.ds(at, PANEL), :] = pm
        lhs = jnp.where(lane >= at + PANEL, pa, 0.0)
        work[...] -= dot(lhs, pa, 0, 0)
        inv[...] -= dot(lhs, pm, 0, 0)
        return carry

    lax.fori_loop(0, n // PANEL, panel, 0)


def left_kernel(
    n_row, n_col, gather, p_ref, left_ref, *rest
):
    if gather:
        half_ref, *rest = rest
    (recv_p, own_p, gpart, recv_g, gown, recv_c, gfull, work, inv1, inv2, half_own,
     sp, rp, sg, rg, sc, rc, sa, ra, sh, rh) = rest
    row, col = lax.axis_index("row"), lax.axis_index("col")
    share = left_ref.shape[0]
    gr = gown.shape[0]
    rank = gfull.shape[0]

    def row_peer(d):
        return lax.rem(row + d, n_row)

    def col_peer(d):
        return lax.rem(col + d, n_col)

    barrier = pltpu.get_barrier_semaphore()
    for d in range(1, n_row):
        pl.semaphore_signal(barrier, inc=1, device_id=(row_peer(d), col), device_id_type=MESH)
    for d in range(1, n_col):
        pl.semaphore_signal(barrier, inc=1, device_id=(row, col_peer(d)), device_id_type=MESH)
    pl.semaphore_wait(barrier, n_row + n_col - 2)

    def remote(src, dst, send, recv, peer):
        c = pltpu.make_async_remote_copy(
            src_ref=src, dst_ref=dst, send_sem=send, recv_sem=recv,
            device_id=peer, device_id_type=MESH,
        )
        c.start()
        return c

    copies = []
    for d in range(1, n_col):
        peer = col_peer(d)
        at = pl.multiple_of(peer * share, 8)
        copies.append(remote(p_ref.at[pl.ds(at, share)], recv_p.at[d - 1], sp.at[d - 1], rp.at[d - 1], (row, peer)))
    total = p_ref[pl.ds(pl.multiple_of(col * share, 8), share), :]
    for d in range(1, n_col):
        copies[d - 1].wait()
        total = total + recv_p[d - 1]
    own_p[...] = total

    gpart[...] = dot(own_p[...], own_p[...], 0, 0)
    copies = []
    for d in range(1, n_row):
        peer = row_peer(d)
        at = pl.multiple_of(peer * gr, 8)
        copies.append(remote(gpart.at[pl.ds(at, gr)], recv_g.at[d - 1], sg.at[d - 1], rg.at[d - 1], (peer, col)))
    mine = pl.multiple_of(row * gr, 8)
    total = gpart[pl.ds(mine, gr), :]
    for d in range(1, n_row):
        copies[d - 1].wait()
        total = total + recv_g[d - 1]
    recv_c[pl.ds(col, 1)] = total[None]
    copies = []
    for d in range(1, n_col):
        copies.append(remote(recv_c.at[col], recv_c.at[col], sc.at[d - 1], rc.at[d - 1], (row, col_peer(d))))
    for c in copies:
        c.wait()
    total = recv_c[0]
    for i in range(1, n_col):
        total = total + recv_c[i]
    gown[...] = total
    gfull[pl.ds(mine, gr), :] = total
    copies = []
    for d in range(1, n_row):
        copies.append(remote(gown, gfull.at[pl.ds(mine, gr)], sa.at[d - 1], ra.at[d - 1], (row_peer(d), col)))
    for c in copies:
        c.wait()

    b = BLOCK
    inverse_factor(gfull[:b, :b], work, inv1)
    l21 = dot(gfull[b:, :b], inv1[...], 1, 1)
    left1 = dot(own_p[:, :b], inv1[...], 1, 1)
    left_ref[:, :b] = left1
    own_p[:, b:] -= dot(left1, l21, 1, 1)
    inverse_factor(gfull[b:, b:] - dot(l21, l21, 1, 1), work, inv2)
    left_ref[:, b:] = dot(own_p[:, b:], inv2[...], 1, 1)
    if gather:
        half = left_ref[...].astype(jnp.bfloat16)
        half_own[...] = half
        at = pl.multiple_of(col * share, 16)
        half_ref[pl.ds(at, share), :] = half
        copies = []
        for d in range(1, n_col):
            copies.append(remote(half_own, half_ref.at[pl.ds(at, share)], sh.at[d - 1], rh.at[d - 1], (row, col_peer(d))))
        for c in copies:
            c.wait()


def left_of(partial, n_row, n_col):
    rows, rank = partial.shape
    share = rows // n_col
    gr = rank // n_row
    gather = share % 16 == 0
    f32 = jnp.float32
    out = [jax.ShapeDtypeStruct((share, rank), f32)]
    if gather:
        out.append(jax.ShapeDtypeStruct((rows, rank), jnp.bfloat16))
    vmem = pl.BlockSpec(memory_space=pltpu.VMEM)
    dma = pltpu.SemaphoreType.DMA
    res = pl.pallas_call(
        functools.partial(left_kernel, n_row, n_col, gather),
        out_shape=out,
        in_specs=[vmem],
        out_specs=[vmem] * len(out),
        scratch_shapes=[
            pltpu.VMEM((n_col - 1, share, rank), f32),
            pltpu.VMEM((share, rank), f32),
            pltpu.VMEM((rank, rank), f32),
            pltpu.VMEM((n_row - 1, gr, rank), f32),
            pltpu.VMEM((gr, rank), f32),
            pltpu.VMEM((n_col, gr, rank), f32),
            pltpu.VMEM((rank, rank), f32),
            pltpu.VMEM((BLOCK, BLOCK), f32),
            pltpu.VMEM((BLOCK, BLOCK), f32),
            pltpu.VMEM((BLOCK, BLOCK), f32),
            pltpu.VMEM((share, rank), jnp.bfloat16),
            dma((n_col - 1,)), dma((n_col - 1,)),
            dma((n_row - 1,)), dma((n_row - 1,)),
            dma((n_col - 1,)), dma((n_col - 1,)),
            dma((n_row - 1,)), dma((n_row - 1,)),
            dma((n_col - 1,)), dma((n_col - 1,)),
        ],
        compiler_params=pltpu.CompilerParams(
            collective_id=0, has_side_effects=True, vmem_limit_bytes=24 * 1024 * 1024
        ),
    )(partial)
    if gather:
        return res
    left = res[0]
    return left, lax.all_gather(left.astype(jnp.bfloat16), "col", axis=0, tiled=True)


def per_device(n_row, n_col, momentum, gradient, basis):
    buffer = (momentum.astype(jnp.float32) + gradient.astype(jnp.float32)).astype(jnp.bfloat16)
    directions = basis.astype(jnp.bfloat16)
    for step in range(POWER):
        partial_value = lax.dot_general(
            buffer,
            lax.all_gather(directions, "row", axis=0, tiled=True),
            (((1,), (1,)), ((), ())),
            preferred_element_type=jnp.float32,
        )
        left_share, left_half = left_of(partial_value, n_row, n_col)
        right_own = lax.psum_scatter(
            lax.dot_general(
                left_half, buffer, (((0,), (0,)), ((), ())), preferred_element_type=jnp.float32
            ),
            "row", scatter_dimension=0, tiled=True,
        )
        directions = right_own.astype(jnp.bfloat16)
    squares = lax.psum(jnp.sum(right_own * right_own, axis=1), "col")
    right_whole = lax.all_gather(directions, "row", axis=0, tiled=True)
    basis_new = right_own / jnp.sqrt(squares[:, None] / COLS + epsilon)
    update = jnp.dot(left_half, right_whole, preferred_element_type=jnp.float32)
    momentum_new = (buffer.astype(jnp.float32) - (1.0 - decay_rate) * update).astype(jnp.bfloat16)
    return (momentum_new, basis_new, left_share)


def solution(mesh):
    return jax.shard_map(
        functools.partial(per_device, mesh.shape["row"], mesh.shape["col"]),
        mesh=mesh,
        in_specs=(P("row", "col"), P("row", "col"), P("row", "col")),
        out_specs=(P("row", "col"), P("row", "col"), P(("row", "col"), None)),
        check_vma=False,
    )
```

```python
import functools

import jax
import jax.numpy as jnp
from jax import lax
from jax.experimental import pallas as pl
from jax.experimental.pallas import tpu as pltpu
from jax.sharding import PartitionSpec as P

COLS = 26624
POWER = 2
BLOCK = 128
PANEL = 16
MESH = pl.DeviceIdType.MESH
HIGHEST = lax.Precision.HIGHEST


decay_rate = 0.95
epsilon = 1e-06


def dot(a, b, ca, cb, precision=HIGHEST):
    return lax.dot_general(
        a, b, (((ca,), (cb,)), ((), ())), precision=precision, preferred_element_type=jnp.float32
    )


def inverse_factor(a, work, inv):
    n = BLOCK
    work[...] = a
    rows = lax.broadcasted_iota(jnp.int32, (n, n), 0)
    lanes = lax.broadcasted_iota(jnp.int32, (n, n), 1)
    inv[...] = jnp.where(rows == lanes, 1.0, 0.0).astype(jnp.float32)
    sub = lax.broadcasted_iota(jnp.int32, (PANEL, n), 0)
    lane = lax.broadcasted_iota(jnp.int32, (PANEL, n), 1)

    def panel(p, carry):
        at = pl.multiple_of(p * PANEL, PANEL)
        pa = work[pl.ds(at, PANEL), :]
        pm = inv[pl.ds(at, PANEL), :]
        d = pltpu.roll(pa, n - at, 1)
        for k in range(PANEL):
            pivot = jnp.broadcast_to(d[k : k + 1, k : k + 1], (PANEL, n))
            r = lax.rsqrt(pivot)
            r = r * (1.5 - 0.5 * (pivot * r) * r)
            column = jnp.broadcast_to(d[:, k : k + 1], (PANEL, n)) * r
            dk = jnp.broadcast_to(d[k : k + 1, :], (PANEL, n)) * r
            ak = jnp.broadcast_to(pa[k : k + 1, :], (PANEL, n)) * r
            mk = jnp.broadcast_to(pm[k : k + 1, :], (PANEL, n)) * r
            below = sub > k
            here = sub == k
            d = jnp.where(here, dk, jnp.where(below, d - column * dk, d))
            pa = jnp.where(here, ak, jnp.where(below, pa - column * ak, pa))
            pm = jnp.where(here, mk, jnp.where(below, pm - column * mk, pm))
        inv[pl.ds(at, PANEL), :] = pm
        lhs = jnp.where(lane >= at + PANEL, pa, 0.0)
        work[...] -= dot(lhs, pa, 0, 0)
        inv[...] -= dot(lhs, pm, 0, 0)
        return carry

    lax.fori_loop(0, n // PANEL, panel, 0)


def left_kernel(
    n_row, n_col, gather, p_ref, left_ref, *rest
):
    if gather:
        half_ref, *rest = rest
    (recv_p, own_p, gpart, recv_g, gown, recv_c, gfull, work, inv1, inv2, half_own,
     sp, rp, sg, rg, sc, rc, sa, ra, sh, rh) = rest
    row, col = lax.axis_index("row"), lax.axis_index("col")
    share = left_ref.shape[0]
    gr = gown.shape[0]
    rank = gfull.shape[0]

    def row_peer(d):
        return lax.rem(row + d, n_row)

    def col_peer(d):
        return lax.rem(col + d, n_col)

    barrier = pltpu.get_barrier_semaphore()
    for d in range(1, n_row):
        pl.semaphore_signal(barrier, inc=1, device_id=(row_peer(d), col), device_id_type=MESH)
    for d in range(1, n_col):
        pl.semaphore_signal(barrier, inc=1, device_id=(row, col_peer(d)), device_id_type=MESH)
    pl.semaphore_wait(barrier, n_row + n_col - 2)

    def remote(src, dst, send, recv, peer):
        c = pltpu.make_async_remote_copy(
            src_ref=src, dst_ref=dst, send_sem=send, recv_sem=recv,
            device_id=peer, device_id_type=MESH,
        )
        c.start()
        return c

    copies = []
    for d in range(1, n_col):
        peer = col_peer(d)
        at = pl.multiple_of(peer * share, 8)
        copies.append(remote(p_ref.at[pl.ds(at, share)], recv_p.at[d - 1], sp.at[d - 1], rp.at[d - 1], (row, peer)))
    total = p_ref[pl.ds(pl.multiple_of(col * share, 8), share), :]
    for d in range(1, n_col):
        copies[d - 1].wait()
        total = total + recv_p[d - 1]
    own_p[...] = total

    gpart[...] = dot(own_p[...], own_p[...], 0, 0)
    copies = []
    for d in range(1, n_row):
        peer = row_peer(d)
        at = pl.multiple_of(peer * gr, 8)
        copies.append(remote(gpart.at[pl.ds(at, gr)], recv_g.at[d - 1], sg.at[d - 1], rg.at[d - 1], (peer, col)))
    mine = pl.multiple_of(row * gr, 8)
    total = gpart[pl.ds(mine, gr), :]
    for d in range(1, n_row):
        copies[d - 1].wait()
        total = total + recv_g[d - 1]
    recv_c[pl.ds(col, 1)] = total[None]
    copies = []
    for d in range(1, n_col):
        copies.append(remote(recv_c.at[col], recv_c.at[col], sc.at[d - 1], rc.at[d - 1], (row, col_peer(d))))
    for c in copies:
        c.wait()
    total = recv_c[0]
    for i in range(1, n_col):
        total = total + recv_c[i]
    gown[...] = total
    gfull[pl.ds(mine, gr), :] = total
    copies = []
    for d in range(1, n_row):
        copies.append(remote(gown, gfull.at[pl.ds(mine, gr)], sa.at[d - 1], ra.at[d - 1], (row_peer(d), col)))
    for c in copies:
        c.wait()

    b = BLOCK
    inverse_factor(gfull[:b, :b], work, inv1)
    l21 = dot(gfull[b:, :b], inv1[...], 1, 1)
    left1 = dot(own_p[:, :b], inv1[...], 1, 1)
    left_ref[:, :b] = left1
    own_p[:, b:] -= dot(left1, l21, 1, 1)
    inverse_factor(gfull[b:, b:] - dot(l21, l21, 1, 1), work, inv2)
    left_ref[:, b:] = dot(own_p[:, b:], inv2[...], 1, 1)
    if gather:
        half = left_ref[...].astype(jnp.bfloat16)
        half_own[...] = half
        at = pl.multiple_of(col * share, 16)
        half_ref[pl.ds(at, share), :] = half
        copies = []
        for d in range(1, n_col):
            copies.append(remote(half_own, half_ref.at[pl.ds(at, share)], sh.at[d - 1], rh.at[d - 1], (row, col_peer(d))))
        for c in copies:
            c.wait()


def left_of(partial, n_row, n_col):
    rows, rank = partial.shape
    share = rows // n_col
    gr = rank // n_row
    gather = share % 16 == 0
    f32 = jnp.float32
    out = [jax.ShapeDtypeStruct((share, rank), f32)]
    if gather:
        out.append(jax.ShapeDtypeStruct((rows, rank), jnp.bfloat16))
    vmem = pl.BlockSpec(memory_space=pltpu.VMEM)
    dma = pltpu.SemaphoreType.DMA
    res = pl.pallas_call(
        functools.partial(left_kernel, n_row, n_col, gather),
        out_shape=out,
        in_specs=[vmem],
        out_specs=[vmem] * len(out),
        scratch_shapes=[
            pltpu.VMEM((n_col - 1, share, rank), f32),
            pltpu.VMEM((share, rank), f32),
            pltpu.VMEM((rank, rank), f32),
            pltpu.VMEM((n_row - 1, gr, rank), f32),
            pltpu.VMEM((gr, rank), f32),
            pltpu.VMEM((n_col, gr, rank), f32),
            pltpu.VMEM((rank, rank), f32),
            pltpu.VMEM((BLOCK, BLOCK), f32),
            pltpu.VMEM((BLOCK, BLOCK), f32),
            pltpu.VMEM((BLOCK, BLOCK), f32),
            pltpu.VMEM((share, rank), jnp.bfloat16),
            dma((n_col - 1,)), dma((n_col - 1,)),
            dma((n_row - 1,)), dma((n_row - 1,)),
            dma((n_col - 1,)), dma((n_col - 1,)),
            dma((n_row - 1,)), dma((n_row - 1,)),
            dma((n_col - 1,)), dma((n_col - 1,)),
        ],
        compiler_params=pltpu.CompilerParams(
            collective_id=0, has_side_effects=True, vmem_limit_bytes=24 * 1024 * 1024
        ),
    )(partial)
    if gather:
        return res
    left = res[0]
    return left, lax.all_gather(left.astype(jnp.bfloat16), "col", axis=0, tiled=True)


def ring_kernel(n_row, part_ref, own_ref, whole_ref, peer_part, out_r, in_r, out_l, in_l,
                xs, xr, rs, rr, ls, lr, gs, gr_, hs, hr, cs, cr):
    row, col = lax.axis_index("row"), lax.axis_index("col")
    chips = n_row // 2
    last = chips - 1
    z, core = lax.div(row, 2), lax.rem(row, 2)
    peer = (z * 2 + 1 - core, col)
    right = (lax.rem(row + 2, n_row), col)
    left = (lax.rem(row + n_row - 2, n_row), col)
    has_right, has_left = z < last, z > 0
    columns = own_ref.shape[1]
    width = 512 if columns % 512 == 0 else 128

    barrier = pltpu.get_barrier_semaphore()
    pl.semaphore_signal(barrier, inc=1, device_id=peer, device_id_type=MESH)

    @pl.when(has_right)
    def _():
        pl.semaphore_signal(barrier, inc=1, device_id=right, device_id_type=MESH)

    @pl.when(has_left)
    def _():
        pl.semaphore_signal(barrier, inc=1, device_id=left, device_id_type=MESH)

    pl.semaphore_wait(barrier, 1 + has_right.astype(jnp.int32) + has_left.astype(jnp.int32))

    def remote(src, dst, send, recv, device):
        return pltpu.make_async_remote_copy(
            src_ref=src, dst_ref=dst, send_sem=send, recv_sem=recv,
            device_id=device, device_id_type=MESH,
        )

    def over_columns(body):
        def step(i, carry):
            body(pl.ds(pl.multiple_of(i * width, width), width))
            return carry

        lax.fori_loop(0, columns // width, step, 0)

    def exchange(t):
        return remote(part_ref.at[t, 1 - core], peer_part.at[t], xs.at[t], xr.at[t], peer)

    order = []
    for k in range(chips):
        for t in (last - k, k):
            if t not in order:
                order.append(t)
    for t in order:
        exchange(t).start()

    def chip_sum(t, at):
        return part_ref[t, core, :, at] + peer_part[t, :, at]

    def to_right(k):
        return remote(out_r.at[k], in_r.at[k], rs.at[k], rr.at[k], right)

    def to_left(k):
        return remote(out_l.at[k], in_l.at[k], ls.at[k], lr.at[k], left)

    arrived = []
    for k in range(last):
        for t, rightward in ((last - k, True), (k, False)):
            if t not in arrived:
                arrived.append(t)
                exchange(t).wait_recv()
            out, into = (out_r, in_r) if rightward else (out_l, in_l)
            copy = to_right(k) if rightward else to_left(k)
            first = z == (0 if rightward else last)
            before = z < t if rightward else z > t
            reached = z <= t if rightward else z >= t

            @pl.when(jnp.logical_and(jnp.logical_not(first), reached))
            def _():
                copy.wait_recv()

            @pl.when(jnp.logical_and(first, before))
            def _():
                def body(at):
                    out[k, :, at] = chip_sum(t, at).astype(jnp.bfloat16)

                over_columns(body)

            @pl.when(jnp.logical_and(jnp.logical_not(first), before))
            def _():
                def body(at):
                    out[k, :, at] = (chip_sum(t, at) + into[k, :, at].astype(jnp.float32)).astype(jnp.bfloat16)

                over_columns(body)

            @pl.when(before)
            def _():
                copy.start()

    for t in range(chips):
        if t not in arrived:
            exchange(t).wait_recv()
    for t in range(chips):
        @pl.when(z == t)
        def _():
            def body(at):
                total = chip_sum(t, at)
                if t > 0:
                    total = total + in_r[last - t, :, at].astype(jnp.float32)
                if t < last:
                    total = total + in_l[t, :, at].astype(jnp.float32)
                own_ref[:, at] = total
                whole_ref[t, core, :, at] = total.astype(jnp.bfloat16)

            over_columns(body)

    def same_place(j, send, recv, device):
        place = whole_ref.at[j, core]
        return remote(place, place, send, recv, device)

    def from_peer(j, send, recv):
        place = whole_ref.at[j, 1 - core]
        return remote(place, place, send, recv, peer)

    same_place(z, cs.at[0], cr.at[0], peer).start()
    for k in range(last):
        @pl.when(jnp.logical_and(has_right, z - k >= 0))
        def _():
            same_place(z - k, gs.at[k], gr_.at[k], right).start()

        @pl.when(jnp.logical_and(has_left, z + k <= last))
        def _():
            same_place(z + k, hs.at[k], hr.at[k], left).start()

        @pl.when(z - 1 - k >= 0)
        def _():
            same_place(z - 1 - k, gs.at[k], gr_.at[k], right).wait_recv()
            same_place(z - 1 - k, cs.at[1 + k], cr.at[1 + k], peer).start()

        @pl.when(z + 1 + k <= last)
        def _():
            same_place(z + 1 + k, hs.at[k], hr.at[k], left).wait_recv()
            same_place(z + 1 + k, cs.at[chips + k], cr.at[chips + k], peer).start()

    from_peer(z, cs.at[0], cr.at[0]).wait_recv()
    same_place(z, cs.at[0], cr.at[0], peer).wait_send()
    for t in order:
        exchange(t).wait_send()
    for k in range(last):
        @pl.when(z < last - k)
        def _():
            to_right(k).wait_send()

        @pl.when(z > k)
        def _():
            to_left(k).wait_send()

        @pl.when(jnp.logical_and(has_right, z - k >= 0))
        def _():
            same_place(z - k, gs.at[k], gr_.at[k], right).wait_send()

        @pl.when(jnp.logical_and(has_left, z + k <= last))
        def _():
            same_place(z + k, hs.at[k], hr.at[k], left).wait_send()

        @pl.when(z - 1 - k >= 0)
        def _():
            same_place(z - 1 - k, cs.at[1 + k], cr.at[1 + k], peer).wait_send()
            from_peer(z - 1 - k, cs.at[1 + k], cr.at[1 + k]).wait_recv()

        @pl.when(z + 1 + k <= last)
        def _():
            same_place(z + 1 + k, cs.at[chips + k], cr.at[chips + k], peer).wait_send()
            from_peer(z + 1 + k, cs.at[chips + k], cr.at[chips + k]).wait_recv()


def right_of(partial, n_row):
    rank, columns = partial.shape
    gr = rank // n_row
    if gr % 16 != 0:
        own = lax.psum_scatter(partial, "row", scatter_dimension=0, tiled=True)
        return own, lax.all_gather(own.astype(jnp.bfloat16), "row", axis=0, tiled=True)
    chips = n_row // 2
    hops = chips - 1
    vmem = pl.BlockSpec(memory_space=pltpu.VMEM)
    dma = pltpu.SemaphoreType.DMA
    wire = pltpu.VMEM((hops, gr, columns), jnp.bfloat16)
    own, whole = pl.pallas_call(
        functools.partial(ring_kernel, n_row),
        out_shape=[
            jax.ShapeDtypeStruct((gr, columns), jnp.float32),
            jax.ShapeDtypeStruct((chips, 2, gr, columns), jnp.bfloat16),
        ],
        in_specs=[vmem],
        out_specs=[vmem, vmem],
        scratch_shapes=[
            pltpu.VMEM((chips, gr, columns), jnp.float32),
            wire, wire, wire, wire,
            dma((chips,)), dma((chips,)),
            dma((hops,)), dma((hops,)), dma((hops,)), dma((hops,)),
            dma((hops,)), dma((hops,)), dma((hops,)), dma((hops,)),
            dma((2 * chips - 1,)), dma((2 * chips - 1,)),
        ],
        compiler_params=pltpu.CompilerParams(
            collective_id=1, has_side_effects=True, vmem_limit_bytes=40 * 1024 * 1024
        ),
    )(partial.reshape(chips, 2, gr, columns))
    return own, whole.reshape(rank, columns)


def per_device(n_row, n_col, momentum, gradient, basis):
    buffer = (momentum.astype(jnp.float32) + gradient.astype(jnp.float32)).astype(jnp.bfloat16)
    whole = lax.all_gather(basis.astype(jnp.bfloat16), "row", axis=0, tiled=True)
    for step in range(POWER):
        partial_value = lax.dot_general(
            buffer, whole, (((1,), (1,)), ((), ())), preferred_element_type=jnp.float32
        )
        left_share, left_half = left_of(partial_value, n_row, n_col)
        right_own, whole = right_of(
            lax.dot_general(
                left_half, buffer, (((0,), (0,)), ((), ())), preferred_element_type=jnp.float32
            ),
            n_row,
        )
    squares = lax.psum(jnp.sum(right_own * right_own, axis=1), "col")
    basis_new = right_own / jnp.sqrt(squares[:, None] / COLS + epsilon)
    update = jnp.dot(left_half, whole, preferred_element_type=jnp.float32)
    momentum_new = (buffer.astype(jnp.float32) - (1.0 - decay_rate) * update).astype(jnp.bfloat16)
    return (momentum_new, basis_new, left_share)


def solution(mesh):
    return jax.shard_map(
        functools.partial(per_device, mesh.shape["row"], mesh.shape["col"]),
        mesh=mesh,
        in_specs=(P("row", "col"), P("row", "col"), P("row", "col")),
        out_specs=(P("row", "col"), P("row", "col"), P(("row", "col"), None)),
        check_vma=False,
    )
```

```python
import functools

import jax
import jax.numpy as jnp
from jax import lax
from jax.experimental import pallas as pl
from jax.experimental.pallas import tpu as pltpu
from jax.sharding import PartitionSpec as P

COLS = 26624
POWER = 2
BLOCK = 128
PANEL = 16
MESH = pl.DeviceIdType.MESH
HIGHEST = lax.Precision.HIGHEST


decay_rate = 0.95
epsilon = 1e-06


def dot(a, b, ca, cb, precision=HIGHEST):
    return lax.dot_general(
        a, b, (((ca,), (cb,)), ((), ())), precision=precision, preferred_element_type=jnp.float32
    )


def inverse_factor(a, work, inv):
    n = BLOCK
    work[...] = a
    rows = lax.broadcasted_iota(jnp.int32, (n, n), 0)
    lanes = lax.broadcasted_iota(jnp.int32, (n, n), 1)
    inv[...] = jnp.where(rows == lanes, 1.0, 0.0).astype(jnp.float32)
    sub = lax.broadcasted_iota(jnp.int32, (PANEL, n), 0)
    lane = lax.broadcasted_iota(jnp.int32, (PANEL, n), 1)

    def panel(p, carry):
        at = pl.multiple_of(p * PANEL, PANEL)
        pa = work[pl.ds(at, PANEL), :]
        pm = inv[pl.ds(at, PANEL), :]
        d = pltpu.roll(pa, n - at, 1)
        for k in range(PANEL):
            pivot = jnp.broadcast_to(d[k : k + 1, k : k + 1], (PANEL, n))
            r = lax.rsqrt(pivot)
            r = r * (1.5 - 0.5 * (pivot * r) * r)
            column = jnp.broadcast_to(d[:, k : k + 1], (PANEL, n)) * r
            dk = jnp.broadcast_to(d[k : k + 1, :], (PANEL, n)) * r
            ak = jnp.broadcast_to(pa[k : k + 1, :], (PANEL, n)) * r
            mk = jnp.broadcast_to(pm[k : k + 1, :], (PANEL, n)) * r
            below = sub > k
            here = sub == k
            d = jnp.where(here, dk, jnp.where(below, d - column * dk, d))
            pa = jnp.where(here, ak, jnp.where(below, pa - column * ak, pa))
            pm = jnp.where(here, mk, jnp.where(below, pm - column * mk, pm))
        inv[pl.ds(at, PANEL), :] = pm
        lhs = jnp.where(lane >= at + PANEL, pa, 0.0)
        work[...] -= dot(lhs, pa, 0, 0)
        inv[...] -= dot(lhs, pm, 0, 0)
        return carry

    lax.fori_loop(0, n // PANEL, panel, 0)


def left_kernel(
    n_row, n_col, gather, p_ref, left_ref, *rest
):
    if gather:
        half_ref, *rest = rest
    (recv_p, own_p, gpart, recv_g, gown, recv_c, gfull, work, inv1, inv2, half_own,
     sp, rp, sg, rg, sc, rc, sa, ra, sh, rh) = rest
    row, col = lax.axis_index("row"), lax.axis_index("col")
    share = left_ref.shape[0]
    gr = gown.shape[0]
    rank = gfull.shape[0]

    def row_peer(d):
        return lax.rem(row + d, n_row)

    def col_peer(d):
        return lax.rem(col + d, n_col)

    barrier = pltpu.get_barrier_semaphore()
    for d in range(1, n_row):
        pl.semaphore_signal(barrier, inc=1, device_id=(row_peer(d), col), device_id_type=MESH)
    for d in range(1, n_col):
        pl.semaphore_signal(barrier, inc=1, device_id=(row, col_peer(d)), device_id_type=MESH)
    pl.semaphore_wait(barrier, n_row + n_col - 2)

    def remote(src, dst, send, recv, peer):
        c = pltpu.make_async_remote_copy(
            src_ref=src, dst_ref=dst, send_sem=send, recv_sem=recv,
            device_id=peer, device_id_type=MESH,
        )
        c.start()
        return c

    copies = []
    for d in range(1, n_col):
        peer = col_peer(d)
        at = pl.multiple_of(peer * share, 8)
        copies.append(remote(p_ref.at[pl.ds(at, share)], recv_p.at[d - 1], sp.at[d - 1], rp.at[d - 1], (row, peer)))
    total = p_ref[pl.ds(pl.multiple_of(col * share, 8), share), :]
    for d in range(1, n_col):
        copies[d - 1].wait()
        total = total + recv_p[d - 1]
    own_p[...] = total

    gpart[...] = dot(own_p[...], own_p[...], 0, 0)
    copies = []
    for d in range(1, n_row):
        peer = row_peer(d)
        at = pl.multiple_of(peer * gr, 8)
        copies.append(remote(gpart.at[pl.ds(at, gr)], recv_g.at[d - 1], sg.at[d - 1], rg.at[d - 1], (peer, col)))
    mine = pl.multiple_of(row * gr, 8)
    total = gpart[pl.ds(mine, gr), :]
    for d in range(1, n_row):
        copies[d - 1].wait()
        total = total + recv_g[d - 1]
    recv_c[pl.ds(col, 1)] = total[None]
    copies = []
    for d in range(1, n_col):
        copies.append(remote(recv_c.at[col], recv_c.at[col], sc.at[d - 1], rc.at[d - 1], (row, col_peer(d))))
    for c in copies:
        c.wait()
    total = recv_c[0]
    for i in range(1, n_col):
        total = total + recv_c[i]
    gown[...] = total
    gfull[pl.ds(mine, gr), :] = total
    copies = []
    for d in range(1, n_row):
        copies.append(remote(gown, gfull.at[pl.ds(mine, gr)], sa.at[d - 1], ra.at[d - 1], (row_peer(d), col)))
    for c in copies:
        c.wait()

    b = BLOCK
    inverse_factor(gfull[:b, :b], work, inv1)
    l21 = dot(gfull[b:, :b], inv1[...], 1, 1)
    left1 = dot(own_p[:, :b], inv1[...], 1, 1)
    left_ref[:, :b] = left1
    own_p[:, b:] -= dot(left1, l21, 1, 1)
    inverse_factor(gfull[b:, b:] - dot(l21, l21, 1, 1), work, inv2)
    left_ref[:, b:] = dot(own_p[:, b:], inv2[...], 1, 1)
    if gather:
        half = left_ref[...].astype(jnp.bfloat16)
        half_own[...] = half
        at = pl.multiple_of(col * share, 16)
        half_ref[pl.ds(at, share), :] = half
        copies = []
        for d in range(1, n_col):
            copies.append(remote(half_own, half_ref.at[pl.ds(at, share)], sh.at[d - 1], rh.at[d - 1], (row, col_peer(d))))
        for c in copies:
            c.wait()


def left_of(partial, n_row, n_col):
    rows, rank = partial.shape
    share = rows // n_col
    gr = rank // n_row
    gather = share % 16 == 0
    f32 = jnp.float32
    out = [jax.ShapeDtypeStruct((share, rank), f32)]
    if gather:
        out.append(jax.ShapeDtypeStruct((rows, rank), jnp.bfloat16))
    vmem = pl.BlockSpec(memory_space=pltpu.VMEM)
    dma = pltpu.SemaphoreType.DMA
    res = pl.pallas_call(
        functools.partial(left_kernel, n_row, n_col, gather),
        out_shape=out,
        in_specs=[vmem],
        out_specs=[vmem] * len(out),
        scratch_shapes=[
            pltpu.VMEM((n_col - 1, share, rank), f32),
            pltpu.VMEM((share, rank), f32),
            pltpu.VMEM((rank, rank), f32),
            pltpu.VMEM((n_row - 1, gr, rank), f32),
            pltpu.VMEM((gr, rank), f32),
            pltpu.VMEM((n_col, gr, rank), f32),
            pltpu.VMEM((rank, rank), f32),
            pltpu.VMEM((BLOCK, BLOCK), f32),
            pltpu.VMEM((BLOCK, BLOCK), f32),
            pltpu.VMEM((BLOCK, BLOCK), f32),
            pltpu.VMEM((share, rank), jnp.bfloat16),
            dma((n_col - 1,)), dma((n_col - 1,)),
            dma((n_row - 1,)), dma((n_row - 1,)),
            dma((n_col - 1,)), dma((n_col - 1,)),
            dma((n_row - 1,)), dma((n_row - 1,)),
            dma((n_col - 1,)), dma((n_col - 1,)),
        ],
        compiler_params=pltpu.CompilerParams(
            collective_id=0, has_side_effects=True, vmem_limit_bytes=24 * 1024 * 1024
        ),
    )(partial)
    if gather:
        return res
    left = res[0]
    return left, lax.all_gather(left.astype(jnp.bfloat16), "col", axis=0, tiled=True)


def ring_kernel(n_row, part_ref, own_ref, whole_ref, peer_part, out_r, in_r, out_l, in_l,
                xs, xr, rs, rr, ls, lr, gs, gr_, hs, hr, cs, cr):
    row, col = lax.axis_index("row"), lax.axis_index("col")
    chips = n_row // 2
    last = chips - 1
    z, core = lax.div(row, 2), lax.rem(row, 2)
    peer = (z * 2 + 1 - core, col)
    right = (lax.rem(row + 2, n_row), col)
    left = (lax.rem(row + n_row - 2, n_row), col)
    has_right, has_left = z < last, z > 0
    columns = own_ref.shape[1]
    width = 512 if columns % 512 == 0 else 128

    barrier = pltpu.get_barrier_semaphore()
    pl.semaphore_signal(barrier, inc=1, device_id=peer, device_id_type=MESH)

    @pl.when(has_right)
    def _():
        pl.semaphore_signal(barrier, inc=1, device_id=right, device_id_type=MESH)

    @pl.when(has_left)
    def _():
        pl.semaphore_signal(barrier, inc=1, device_id=left, device_id_type=MESH)

    pl.semaphore_wait(barrier, 1 + has_right.astype(jnp.int32) + has_left.astype(jnp.int32))

    def remote(src, dst, send, recv, device):
        return pltpu.make_async_remote_copy(
            src_ref=src, dst_ref=dst, send_sem=send, recv_sem=recv,
            device_id=device, device_id_type=MESH,
        )

    def over_columns(body):
        def step(i, carry):
            body(pl.ds(pl.multiple_of(i * width, width), width))
            return carry

        lax.fori_loop(0, columns // width, step, 0)

    def exchange(t):
        return remote(part_ref.at[t, 1 - core], peer_part.at[t], xs.at[t], xr.at[t], peer)

    order = []
    for k in range(chips):
        for t in (last - k, k):
            if t not in order:
                order.append(t)
    for t in order:
        exchange(t).start()

    def chip_sum(t, at):
        return part_ref[t, core, :, at] + peer_part[t, :, at]

    def to_right(k):
        return remote(out_r.at[k], in_r.at[k], rs.at[k], rr.at[k], right)

    def to_left(k):
        return remote(out_l.at[k], in_l.at[k], ls.at[k], lr.at[k], left)

    def hop(k, t, rightward, turn):
        out, into = (out_r, in_r) if rightward else (out_l, in_l)
        copy = to_right(k) if rightward else to_left(k)
        first = z == (0 if rightward else last)
        before = jnp.logical_and(turn, z < t if rightward else z > t)
        reached = jnp.logical_and(turn, z <= t if rightward else z >= t)

        @pl.when(jnp.logical_and(jnp.logical_not(first), reached))
        def _():
            copy.wait_recv()

        @pl.when(jnp.logical_and(first, before))
        def _():
            def body(at):
                out[k, :, at] = chip_sum(t, at).astype(jnp.bfloat16)

            over_columns(body)

        @pl.when(jnp.logical_and(jnp.logical_not(first), before))
        def _():
            def body(at):
                out[k, :, at] = (chip_sum(t, at) + into[k, :, at].astype(jnp.float32)).astype(jnp.bfloat16)

            over_columns(body)

        @pl.when(before)
        def _():
            copy.start()

    lower = z < chips // 2
    upper = jnp.logical_not(lower)
    arrived = []
    for k in range(last):
        for t in (last - k, k):
            if t not in arrived:
                arrived.append(t)
                exchange(t).wait_recv()
        hop(k, last - k, True, lower)
        hop(k, k, False, z >= 0)
        hop(k, last - k, True, upper)

    for t in range(chips):
        if t not in arrived:
            exchange(t).wait_recv()
    for t in range(chips):
        @pl.when(z == t)
        def _():
            def body(at):
                total = chip_sum(t, at)
                if t > 0:
                    total = total + in_r[last - t, :, at].astype(jnp.float32)
                if t < last:
                    total = total + in_l[t, :, at].astype(jnp.float32)
                own_ref[:, at] = total
                whole_ref[t, core, :, at] = total.astype(jnp.bfloat16)

            over_columns(body)

    def same_place(j, send, recv, device):
        place = whole_ref.at[j, core]
        return remote(place, place, send, recv, device)

    def from_peer(j, send, recv):
        place = whole_ref.at[j, 1 - core]
        return remote(place, place, send, recv, peer)

    same_place(z, cs.at[0], cr.at[0], peer).start()
    for k in range(last):
        @pl.when(jnp.logical_and(has_right, z - k >= 0))
        def _():
            same_place(z - k, gs.at[k], gr_.at[k], right).start()

        @pl.when(jnp.logical_and(has_left, z + k <= last))
        def _():
            same_place(z + k, hs.at[k], hr.at[k], left).start()

        @pl.when(z - 1 - k >= 0)
        def _():
            same_place(z - 1 - k, gs.at[k], gr_.at[k], right).wait_recv()
            same_place(z - 1 - k, cs.at[1 + k], cr.at[1 + k], peer).start()

        @pl.when(z + 1 + k <= last)
        def _():
            same_place(z + 1 + k, hs.at[k], hr.at[k], left).wait_recv()
            same_place(z + 1 + k, cs.at[chips + k], cr.at[chips + k], peer).start()

    from_peer(z, cs.at[0], cr.at[0]).wait_recv()
    same_place(z, cs.at[0], cr.at[0], peer).wait_send()
    for t in order:
        exchange(t).wait_send()
    for k in range(last):
        @pl.when(z < last - k)
        def _():
            to_right(k).wait_send()

        @pl.when(z > k)
        def _():
            to_left(k).wait_send()

        @pl.when(jnp.logical_and(has_right, z - k >= 0))
        def _():
            same_place(z - k, gs.at[k], gr_.at[k], right).wait_send()

        @pl.when(jnp.logical_and(has_left, z + k <= last))
        def _():
            same_place(z + k, hs.at[k], hr.at[k], left).wait_send()

        @pl.when(z - 1 - k >= 0)
        def _():
            same_place(z - 1 - k, cs.at[1 + k], cr.at[1 + k], peer).wait_send()
            from_peer(z - 1 - k, cs.at[1 + k], cr.at[1 + k]).wait_recv()

        @pl.when(z + 1 + k <= last)
        def _():
            same_place(z + 1 + k, cs.at[chips + k], cr.at[chips + k], peer).wait_send()
            from_peer(z + 1 + k, cs.at[chips + k], cr.at[chips + k]).wait_recv()


def right_of(partial, n_row):
    rank, columns = partial.shape
    gr = rank // n_row
    if gr % 16 != 0:
        own = lax.psum_scatter(partial, "row", scatter_dimension=0, tiled=True)
        return own, lax.all_gather(own.astype(jnp.bfloat16), "row", axis=0, tiled=True)
    chips = n_row // 2
    hops = chips - 1
    vmem = pl.BlockSpec(memory_space=pltpu.VMEM)
    dma = pltpu.SemaphoreType.DMA
    wire = pltpu.VMEM((hops, gr, columns), jnp.bfloat16)
    own, whole = pl.pallas_call(
        functools.partial(ring_kernel, n_row),
        out_shape=[
            jax.ShapeDtypeStruct((gr, columns), jnp.float32),
            jax.ShapeDtypeStruct((chips, 2, gr, columns), jnp.bfloat16),
        ],
        in_specs=[vmem],
        out_specs=[vmem, vmem],
        scratch_shapes=[
            pltpu.VMEM((chips, gr, columns), jnp.float32),
            wire, wire, wire, wire,
            dma((chips,)), dma((chips,)),
            dma((hops,)), dma((hops,)), dma((hops,)), dma((hops,)),
            dma((hops,)), dma((hops,)), dma((hops,)), dma((hops,)),
            dma((2 * chips - 1,)), dma((2 * chips - 1,)),
        ],
        compiler_params=pltpu.CompilerParams(
            collective_id=1, has_side_effects=True, vmem_limit_bytes=40 * 1024 * 1024
        ),
    )(partial.reshape(chips, 2, gr, columns))
    return own, whole.reshape(rank, columns)


def per_device(n_row, n_col, momentum, gradient, basis):
    buffer = (momentum.astype(jnp.float32) + gradient.astype(jnp.float32)).astype(jnp.bfloat16)
    whole = lax.all_gather(basis.astype(jnp.bfloat16), "row", axis=0, tiled=True)
    for step in range(POWER):
        partial_value = lax.dot_general(
            buffer, whole, (((1,), (1,)), ((), ())), preferred_element_type=jnp.float32
        )
        left_share, left_half = left_of(partial_value, n_row, n_col)
        right_own, whole = right_of(
            lax.dot_general(
                left_half, buffer, (((0,), (0,)), ((), ())), preferred_element_type=jnp.float32
            ),
            n_row,
        )
    squares = lax.psum(jnp.sum(right_own * right_own, axis=1), "col")
    basis_new = right_own / jnp.sqrt(squares[:, None] / COLS + epsilon)
    update = jnp.dot(left_half, whole, preferred_element_type=jnp.float32)
    momentum_new = (buffer.astype(jnp.float32) - (1.0 - decay_rate) * update).astype(jnp.bfloat16)
    return (momentum_new, basis_new, left_share)


def solution(mesh):
    return jax.shard_map(
        functools.partial(per_device, mesh.shape["row"], mesh.shape["col"]),
        mesh=mesh,
        in_specs=(P("row", "col"), P("row", "col"), P("row", "col")),
        out_specs=(P("row", "col"), P("row", "col"), P(("row", "col"), None)),
        check_vma=False,
    )
```
